128 devices in a mesh: prow: 8 (over y, z_hi), pcol: 16 (over z_lo, x, core).
Axes of the slice: x: 4, y: 4, z: 4 (z_hi: 2, z_lo: 2; z = z_hi * 2 + z_lo), core: 2. Of those that a mesh axis runs over, the one named last changes fastest.
Arguments:
- factors: bfloat16 [8, 2048, 1024], P('prow', 'pcol'), may hold values from -0.1875 to 0.1875
- shift: float32 [8, 2048], P('prow'), may hold values from 0.5 to 4
Outputs:
- factored: float32 [8, 2048, 16, 1024], P('prow', None, 'pcol')
The draws below stay inside these ranges and needn't reach their ends.
All inputs are finite; a program needn't handle non-finite values.
Results may differ from the reference program's by a relative error of at most 0.0003.
Values may be sent and summed in bfloat16 or wider, within the bound.
No kernel may reach another device: no remote copies, remote signals or barrier semaphores. Data moves between devices by JAX's collectives and lax.ppermute only.
A program may use at most 128 MiB of HBM per device.

```python
import math
import jax
import jax.numpy as jnp
from jax import lax

NB = 256
R = 1024
TC = 4
TR = 8
OWN = 2048
M = 16384
N_PROW = 8
N_PCOL = 16


def block_levels(rng, extent, split, low, high):
    factor_of, own = 1.0, jax.random.fold_in(rng, 6)
    for axis_at, parts in split:
        steps = jnp.exp(jax.random.uniform(jax.random.fold_in(own, axis_at), (parts,), jnp.float32, low / len(split), high / len(split)))
        factor_of = factor_of * jnp.repeat(steps, extent[axis_at] // parts).reshape([-1 if axis == axis_at else 1 for axis in range(len(extent))])
    return factor_of


def noise(key, extent, deviation, most, split=(), kind=jnp.bfloat16):
    gain = block_levels(key, extent, split, -0.22, 0.18) if split else 1.0
    values = jax.random.normal(key, extent, jnp.float32) * deviation * gain
    return jnp.minimum(jnp.maximum(values, -most), most).astype(kind)


def setup_inputs(seed: int = 0) -> dict:
    streams_of = jax.random.split(jax.random.key(seed), 3)
    return {
        "factors": noise(streams_of[0], (N_PROW, OWN, R), R ** -0.5, 0.1875, ((0, 8), (1, 16))),
        "shift": jnp.clip(jnp.exp(math.log(4.0) - 2.0794415 * jax.random.uniform(streams_of[1], (N_PROW, OWN), jnp.float32) ** block_levels(streams_of[1], (N_PROW, OWN), ((0, 8),), -0.2, 0.2)), 0.5, 4.0),
    }


def reference(factors, shift):
    rows_all = factors.reshape(N_PROW, TR, NB, R).transpose(1, 0, 2, 3).reshape(M, R)
    shift_all = shift.reshape(N_PROW, TR, NB).transpose(1, 0, 2).reshape(M)
    schur = jnp.dot(rows_all.astype(jnp.float32), rows_all.T.astype(jnp.float32), preferred_element_type=jnp.float32)
    index_all = jnp.arange(M, dtype=jnp.int32)
    schur = schur.at[index_all, index_all].add(shift_all)
    diagonal_factor = jnp.linalg.cholesky(schur[:NB, :NB])
    below = lax.linalg.triangular_solve(diagonal_factor, schur[NB:, :NB], left_side=False, lower=True, transpose_a=True)
    panel = jnp.concatenate([diagonal_factor, below], axis=0)
    result = schur - jnp.dot(panel, panel.T, precision=lax.Precision.HIGHEST)
    result = result.at[:NB, :].set(schur[:NB, :])
    result = result.at[:, :NB].set(panel)
    result = result.reshape(TR, N_PROW, NB, TC, N_PCOL, NB).transpose(1, 0, 2, 4, 3, 5)
    return result.reshape(N_PROW, OWN, N_PCOL, TC * NB)
```

```python
import jax
import jax.numpy as jnp
from jax import lax
from jax.experimental import pallas as pl
from jax.experimental.pallas import tpu as pltpu
from jax.sharding import PartitionSpec as P

NB = 256
OB = 32
SHARD = 128
R = 1024
TILES = 8
NPCOL = 16
f32 = jnp.float32
bf16 = jnp.bfloat16
HIGHEST = lax.Precision.HIGHEST
NT = (((1,), (1,)), ((), ()))
NN = (((1,), (0,)), ((), ()))
TN = (((0,), (0,)), ((), ()))


def device_of(y, zh, zl, x, core):
    return ((y * 2 + zh) * NPCOL) + (zl * 4 + x) * 2 + core


def every():
    return [
        (y, zh, zl, x, core)
        for y in range(4) for zh in range(2) for zl in range(2) for x in range(4) for core in range(2)
    ]


def moves(step):
    return [(device_of(*at), device_of(*step(*at))) for at in every()]


def along_x(d):
    return moves(lambda y, zh, zl, x, core: (y, zh, zl, (x + d) % 4, core))


def along_y(d):
    return moves(lambda y, zh, zl, x, core: ((y + d) % 4, zh, zl, x, core))


def swap_zl():
    return moves(lambda y, zh, zl, x, core: (y, zh, 1 - zl, x, core))


def swap_zh():
    return moves(lambda y, zh, zl, x, core: (y, 1 - zh, zl, x, core))


def swap_core():
    return moves(lambda y, zh, zl, x, core: (y, zh, zl, x, 1 - core))


def to_columns():
    pairs = []
    for p in range(8):
        for j in range(NPCOL):
            c, b, h = j // 4, j // 2 % 2, j % 2
            pairs.append((p * NPCOL + j, (2 * c + h) * NPCOL + 8 * b + p))
    return pairs


def hop(at, axis, d):
    y, zh, zl, x, core = at
    if axis == "x":
        return (y, zh, zl, (x + d) % 4, core)
    if axis == "y":
        return ((y + d) % 4, zh, zl, x, core)
    z = (zh * 2 + zl + d) % 4
    return (y, z // 2, z % 2, x, core)


def spread_rounds():
    held = {0: [(0, 0, 0, 0, 0)], 1: [(0, 0, 0, 0, 1)]}
    order = {0: "xyz", 1: "yzx"}
    rounds = []
    for step in range(3):
        ops = []
        fresh = {0: [], 1: []}
        for d in (1, 3, 2):
            pairs = []
            for core in range(2):
                for at in held[core]:
                    to = hop(at, order[core][step], d)
                    pairs.append((device_of(*at), device_of(*to)))
                    fresh[core].append(to)
            ops.append(pairs)
        for core in range(2):
            held[core] = held[core] + fresh[core]
        rounds.append(ops)
    return rounds


def split(x):
    hi = x.astype(bf16)
    return hi, (x - hi.astype(f32)).astype(bf16)


def dot(a, b, dims):
    return lax.dot_general(a, b, dims, preferred_element_type=f32)


def factor_rows(a):
    for k0 in range(0, NB, OB):
        for k in range(k0, k0 + OB, 8):
            m = k0 + OB - k
            rows = a[pl.ds(k, m), :]
            cols = [jnp.broadcast_to(rows[:, k + j:k + j + 1], (m, 128)) for j in range(8)]
            sub = lax.broadcasted_iota(jnp.int32, (m, 128), 0)
            done = []
            for j in range(8):
                scale = lax.rsqrt(jnp.broadcast_to(cols[j][j:j + 1, :], (m, 128)))
                u = cols[j] * scale
                for l in range(j + 1, 8):
                    cols[l] = cols[l] - u * jnp.broadcast_to(u[l:l + 1, :], (m, 128))
                row = jnp.concatenate(
                    [rows[j:j + 1, 128 * c:128 * c + 128] * scale[0:1, :] for c in range(4)], 1
                )
                done.append(row)
                below = jnp.where(sub > j, u, 0.0)
                rows = rows - jnp.concatenate(
                    [below * jnp.broadcast_to(row[:, 128 * c:128 * c + 128], (m, 128)) for c in range(4)], 1
                )
            a[pl.ds(k, 8), :] = jnp.concatenate(done, 0)
            if m > 8:
                a[pl.ds(k + 8, m - 8), :] = rows[8:]
        if k0 + OB < NB:
            top = a[pl.ds(k0, OB), :]
            lo = (k0 + OB) // 128 * 128
            update = lax.dot_general(
                top[:, lo:NB], top, TN, preferred_element_type=f32, precision=HIGHEST
            )
            a[pl.ds(k0 + OB, NB - k0 - OB), :] -= update[k0 + OB - lo:]


def factor_kernel(core_ref, own_ref, other_ref, chol_ref, ghi_ref, glo_ref, lead, a):
    core = core_ref[0]
    lead[pl.ds(pl.multiple_of(core * SHARD, SHARD), SHARD), :] = own_ref[:SHARD, :]
    lead[pl.ds(pl.multiple_of((1 - core) * SHARD, SHARD), SHARD), :] = other_ref[:SHARD, :]
    coded = own_ref[SHARD:SHARD + 16, :].astype(f32)[0:1, :]
    shift = coded[:, :NB] + coded[:, NB:2 * NB] + coded[:, 2 * NB:3 * NB]
    row = lax.broadcasted_iota(jnp.int32, (NB, NB), 0)
    col = lax.broadcasted_iota(jnp.int32, (NB, NB), 1)
    f0 = lead[...]
    a[:, :NB] = dot(f0, f0, NT) + jnp.where(row == col, shift, 0.0)
    a[:, NB:] = jnp.where(row == col, 1.0, 0.0)
    factor_rows(a)
    chol_ref[...] = jnp.where(col >= row, a[:, :NB], 0.0)
    whi, wlo = split(a[:, NB:])
    g = dot(whi, f0, NN) + dot(wlo, f0, NN)
    ghi, glo = split(g)
    ghi_ref[...] = ghi
    glo_ref[...] = glo


def factor(core, own, other):
    vm = pl.BlockSpec(memory_space=pltpu.VMEM)
    return pl.pallas_call(
        factor_kernel,
        out_shape=[
            jax.ShapeDtypeStruct((NB, NB), f32),
            jax.ShapeDtypeStruct((NB, R), bf16),
            jax.ShapeDtypeStruct((NB, R), bf16),
        ],
        in_specs=[pl.BlockSpec(memory_space=pltpu.SMEM), vm, vm],
        out_specs=[vm, vm, vm],
        scratch_shapes=[pltpu.VMEM((NB, R), bf16), pltpu.VMEM((NB, 2 * NB), f32)],
        compiler_params=pltpu.CompilerParams(vmem_limit_bytes=32 << 20),
    )(core, own, other)


def tail_kernel(at_ref, *refs):
    fs = refs[0:8]
    cs = refs[8:12]
    shift_ref, chol_ref, ghi_ref, glo_ref, out_ref, f, a, hhi, hlo, sem = refs[12:]
    p, q = at_ref[0], at_ref[1]
    y, zh = p // 2, p % 2
    zl, x, core = q // 8, q // 2 % 4, q % 2
    g = pl.program_id(0)

    def copies():
        out = []
        for n, d in enumerate((0, 1, 3, 2)):
            for dz in range(2):
                for own in range(2):
                    tile = (zl + dz) % 2 * 4 + (x - d + 4) % 4
                    shard = tile * 2 + (core + own) % 2
                    out.append(pltpu.make_async_copy(
                        fs[n * 2 + own].at[dz],
                        f.at[pl.ds(pl.multiple_of(shard * SHARD, SHARD), SHARD), :],
                        sem.at[0],
                    ))
                row = (y - d + 4) % 4 * 2 + (zh + dz) % 2
                out.append(pltpu.make_async_copy(
                    cs[n].at[dz],
                    a.at[pl.ds(pl.multiple_of(row * SHARD, SHARD), SHARD), :],
                    sem.at[0],
                ))
        return out

    @pl.when(g == 0)
    def _():
        for copy in copies():
            copy.start()
        for copy in copies():
            copy.wait()
        for c in range(4):
            at = pl.ds(c * NB, NB)
            ac = a[at, :]
            lhi, llo = split(dot(ac, ghi_ref[...], NT) + dot(ac, glo_ref[...], NT))
            h = ac.astype(f32) - (
                dot(lhi, ghi_ref[...], NN) + dot(lhi, glo_ref[...], NN) + dot(llo, ghi_ref[...], NN)
            )
            hi, lo = split(h)
            hhi[at, :] = hi
            hlo[at, :] = lo

        @pl.when(q == 0)
        def _():
            hhi[pl.ds(0, NB), :] = ghi_ref[...]
            hlo[pl.ds(0, NB), :] = glo_ref[...]

    ft = f[pl.ds(pl.multiple_of(g * NB, NB), NB), :]
    leading = (g == 0) & (p == 0)
    row = lax.broadcasted_iota(jnp.int32, (NB, NB), 0)
    col = lax.broadcasted_iota(jnp.int32, (NB, NB), 1)
    shift = shift_ref[pl.ds(g, 1), :]
    for c in range(4):
        at = pl.ds(c * NB, NB)
        ours = (p == q % 8) & (g == 2 * c + q // 8)
        diagonal = jnp.where((row == col) & ours, shift, 0.0)

        def put(value):
            for n in range(2):
                out_ref[:, 2 * c + n, :] = value[:, n * 128:n * 128 + 128]

        @pl.when(leading)
        def _():
            put(dot(ft, a[at, :], NT) + diagonal)

        @pl.when(jnp.logical_not(leading))
        def _():
            put(dot(ft, hhi[at, :], NT) + dot(ft, hlo[at, :], NT) + diagonal)

    @pl.when(leading & (q == 0))
    def _():
        lower = chol_ref[...].T
        for n in range(2):
            out_ref[:, n, :] = lower[:, n * 128:n * 128 + 128]


def tail(at, fs, cs, shift, chol, ghi, glo):
    hbm = pl.BlockSpec(memory_space=pl.ANY)
    vm = pl.BlockSpec(memory_space=pltpu.VMEM)
    return pl.pallas_call(
        tail_kernel,
        grid=(TILES,),
        out_shape=jax.ShapeDtypeStruct((TILES * NB, 8, 128), f32),
        in_specs=[pl.BlockSpec(memory_space=pltpu.SMEM)] + [hbm] * 12 + [vm] * 4,
        out_specs=pl.BlockSpec((NB, 8, 128), lambda g: (g, 0, 0)),
        scratch_shapes=[
            pltpu.VMEM((TILES * NB, R), bf16),
            pltpu.VMEM((4 * NB, R), bf16),
            pltpu.VMEM((4 * NB, R), bf16),
            pltpu.VMEM((4 * NB, R), bf16),
            pltpu.SemaphoreType.DMA((1,)),
        ],
        compiler_params=pltpu.CompilerParams(vmem_limit_bytes=40 << 20),
    )(at, *fs, *cs, shift, chol, ghi, glo)


def local(factors, shift):
    both = ("prow", "pcol")
    p = lax.axis_index("prow")
    q = lax.axis_index("pcol")
    own = factors[0]

    def send(value, pairs):
        return lax.ppermute(value, both, pairs)

    s = shift[:, :NB]
    s0 = lax.reduce_precision(s, 8, 7)
    s1 = lax.reduce_precision(s - s0, 8, 7)
    s2 = s - s0 - s1
    coded = jnp.concatenate([s0, s1, s2, jnp.zeros_like(s)], 1).astype(bf16)
    lead = jnp.concatenate([own, coded, jnp.zeros((15, R), bf16)], 0)
    lead = jnp.where((p == 0) & (q < 2), lead, jnp.zeros_like(lead))
    for ops in spread_rounds():
        got = [send(lead, pairs) for pairs in ops]
        lead = lead + (got[0] + got[1] + got[2])
    lead_other = send(lead, swap_core())
    chol, ghi, glo = factor(q[None] % 2, lead, lead_other)

    pair = jnp.stack([own, send(own, swap_zl())])
    rows = [pair] + [send(pair, along_x(d)) for d in (1, 3, 2)]
    fs = []
    for value in rows:
        fs += [value, send(value, swap_core())]

    piece = send(own, to_columns())
    piece = jnp.stack([piece, send(piece, swap_zh())])
    cs = [piece] + [send(piece, along_y(d)) for d in (1, 3, 2)]

    out = tail(jnp.stack([p, q]), fs, cs, shift.reshape(TILES, NB), chol, ghi, glo)
    return out.reshape(1, TILES * NB, 1, 4 * NB)


def solution(mesh):
    in_specs = (P("prow", "pcol", None), P("prow", None))
    out_specs = P("prow", None, "pcol", None)
    return jax.shard_map(local, mesh=mesh, in_specs=in_specs, out_specs=out_specs, check_vma=False)
```

```python
import jax
import jax.numpy as jnp
from jax import lax
from jax.experimental import pallas as pl
from jax.experimental.pallas import tpu as pltpu
from jax.sharding import PartitionSpec as P

NB = 256
OB = 32
SHARD = 128
R = 1024
TILES = 8
NPCOL = 16
MB = 512
MSG = R + 384
STEPS = TILES * NB // MB
f32 = jnp.float32
bf16 = jnp.bfloat16
HIGHEST = lax.Precision.HIGHEST
NT = (((1,), (1,)), ((), ()))
NN = (((1,), (0,)), ((), ()))
TN = (((0,), (0,)), ((), ()))


def device_of(y, zh, zl, x, core):
    return ((y * 2 + zh) * NPCOL) + (zl * 4 + x) * 2 + core


def every():
    return [
        (y, zh, zl, x, core)
        for y in range(4) for zh in range(2) for zl in range(2) for x in range(4) for core in range(2)
    ]


def moves(step):
    return [(device_of(*at), device_of(*step(*at))) for at in every()]


def moves(step):
    return [(device_of(*at), device_of(*step(at))) for at in every()]


def swap_zl(at):
    y, zh, zl, x, core = at
    return (y, zh, 1 - zl, x, core)


def swap_zh(at):
    y, zh, zl, x, core = at
    return (y, 1 - zh, zl, x, core)


def swap_core(at):
    y, zh, zl, x, core = at
    return (y, zh, zl, x, 1 - core)


def to_columns():
    pairs = []
    for p in range(8):
        for j in range(NPCOL):
            c, b, h = j // 4, j // 2 % 2, j % 2
            pairs.append((p * NPCOL + j, (2 * c + h) * NPCOL + 8 * b + p))
    return pairs


def hop(at, axis, d):
    y, zh, zl, x, core = at
    if axis == "x":
        return (y, zh, zl, (x + d) % 4, core)
    if axis == "y":
        return ((y + d) % 4, zh, zl, x, core)
    z = (zh * 2 + zl + d) % 4
    return (y, z // 2, z % 2, x, core)


def spread_rounds():
    held = {0: [(0, 0, 0, 0, 0)], 1: [(0, 0, 0, 0, 1)]}
    order = {0: "xyz", 1: "yzx"}
    rounds = []
    for step in range(3):
        ops = []
        fresh = {0: [], 1: []}
        for d in (1, 3, 2):
            pairs = []
            for core in range(2):
                for at in held[core]:
                    to = hop(at, order[core][step], d)
                    pairs.append((device_of(*at), device_of(*to)))
                    fresh[core].append(to)
            ops.append(pairs)
        for core in range(2):
            held[core] = held[core] + fresh[core]
        rounds.append(ops)
    return rounds


def split(x):
    hi = x.astype(bf16)
    return hi, (x - hi.astype(f32)).astype(bf16)


def dot(a, b, dims):
    return lax.dot_general(a, b, dims, preferred_element_type=f32)


def factor_rows(a):
    for k0 in range(0, NB, OB):
        for k in range(k0, k0 + OB, 8):
            m = k0 + OB - k
            rows = a[pl.ds(k, m), :]
            cols = [jnp.broadcast_to(rows[:, k + j:k + j + 1], (m, 128)) for j in range(8)]
            sub = lax.broadcasted_iota(jnp.int32, (m, 128), 0)
            done = []
            for j in range(8):
                scale = lax.rsqrt(jnp.broadcast_to(cols[j][j:j + 1, :], (m, 128)))
                u = cols[j] * scale
                for l in range(j + 1, 8):
                    cols[l] = cols[l] - u * jnp.broadcast_to(u[l:l + 1, :], (m, 128))
                row = jnp.concatenate(
                    [rows[j:j + 1, 128 * c:128 * c + 128] * scale[0:1, :] for c in range(4)], 1
                )
                done.append(row)
                below = jnp.where(sub > j, u, 0.0)
                rows = rows - jnp.concatenate(
                    [below * jnp.broadcast_to(row[:, 128 * c:128 * c + 128], (m, 128)) for c in range(4)], 1
                )
            a[pl.ds(k, 8), :] = jnp.concatenate(done, 0)
            if m > 8:
                a[pl.ds(k + 8, m - 8), :] = rows[8:]
        if k0 + OB < NB:
            top = a[pl.ds(k0, OB), :]
            lo = (k0 + OB) // 128 * 128
            update = lax.dot_general(
                top[:, lo:NB], top, TN, preferred_element_type=f32, precision=HIGHEST
            )
            a[pl.ds(k0 + OB, NB - k0 - OB), :] -= update[k0 + OB - lo:]


def factor_kernel(at_ref, own_ref, other_ref, shift_ref, chol_ref, msg_ref, lead, a):
    p, q = at_ref[0], at_ref[1]
    core = q % 2
    lead[pl.ds(pl.multiple_of(core * SHARD, SHARD), SHARD), :] = own_ref[...]
    lead[pl.ds(pl.multiple_of((1 - core) * SHARD, SHARD), SHARD), :] = other_ref[...]
    row = lax.broadcasted_iota(jnp.int32, (NB, NB), 0)
    col = lax.broadcasted_iota(jnp.int32, (NB, NB), 1)
    f0 = lead[...]
    a[:, :NB] = dot(f0, f0, NT) + jnp.where(row == col, shift_ref[...], 0.0)
    a[:, NB:] = jnp.where(row == col, 1.0, 0.0)
    factor_rows(a)
    chol_ref[...] = jnp.where(col >= row, a[:, :NB], 0.0)
    keep = (p == 0) & (q < 2)
    msg_ref[:, :R] = jnp.where(keep, own_ref[...], jnp.zeros_like(own_ref))
    whi, wlo = split(a[:, NB:])
    part = jnp.where(keep, jnp.where(core == 0, whi, wlo), jnp.zeros_like(whi))
    msg_ref[:, R:R + 128] = part[:128, :128]
    msg_ref[:, R + 128:R + 384] = part[128:, :]


def factor(at, own, other, shift):
    vm = pl.BlockSpec(memory_space=pltpu.VMEM)
    return pl.pallas_call(
        factor_kernel,
        out_shape=[jax.ShapeDtypeStruct((NB, NB), f32), jax.ShapeDtypeStruct((SHARD, MSG), bf16)],
        in_specs=[pl.BlockSpec(memory_space=pltpu.SMEM), vm, vm, vm],
        out_specs=[vm, vm],
        scratch_shapes=[pltpu.VMEM((NB, R), bf16), pltpu.VMEM((NB, 2 * NB), f32)],
        compiler_params=pltpu.CompilerParams(vmem_limit_bytes=32 << 20),
        cost_estimate=pl.CostEstimate(flops=20_000_000_000, bytes_accessed=1 << 20, transcendentals=0),
    )(at, own, other, shift)


def tail_kernel(at_ref, *refs):
    mine, theirs, cols = refs[0:4], refs[4:8], refs[8:12]
    lead_ref, other_ref, shift_ref, chol_ref, out_ref, f, a, hhi, hlo, f0, w, ghi_ref, glo_ref, stage, sem = refs[12:]
    p, q = at_ref[0], at_ref[1]
    y, zh = p // 2, p % 2
    zl, x, core = q // 8, q // 2 % 4, q % 2
    g = pl.program_id(0)

    def shard(n):
        return pl.ds(pl.multiple_of(n * SHARD, SHARD), SHARD)

    @pl.when(g == 0)
    def _():
        for n, d in enumerate((0, 1, 3, 2)):
            for j in range(2):
                for bufs, whose in ((mine, core), (theirs, 1 - core)):
                    tile = (zl + j) % 2 * 4 + (x + 4 - d) % 4
                    f[shard(tile * 2 + whose), :] = bufs[n][j]
                a[shard((y + 4 - d) % 4 * 2 + (zh + j) % 2), :] = cols[n][j]
        f0[pl.ds(pl.multiple_of(core * SHARD, SHARD), SHARD), :] = lead_ref[:, :R]
        f0[pl.ds(pl.multiple_of((1 - core) * SHARD, SHARD), SHARD), :] = other_ref[:, :R]
        for n, (own, other) in enumerate(((lead_ref, other_ref), (other_ref, lead_ref))):
            part = jnp.where(core == 0, own[:, R:], other[:, R:])
            w[n, :128, :128] = part[:, :128]
            w[n, :128, 128:] = jnp.zeros((128, 128), bf16)
            w[n, 128:, :] = part[:, 128:]
        ghi, glo = split(dot(w[0], f0[...], NN) + dot(w[1], f0[...], NN))
        ghi_ref[...] = ghi
        glo_ref[...] = glo
        lhi, llo = split(dot(a[...], ghi_ref[...], NT) + dot(a[...], glo_ref[...], NT))
        for k in range(4):
            at = pl.ds(k * NB, NB)
            h = a[:, at].astype(f32) - (
                dot(lhi, ghi_ref[:, at], NN) + dot(lhi, glo_ref[:, at], NN) + dot(llo, ghi_ref[:, at], NN)
            )
            hi, lo = split(h)
            hhi[:, at] = hi
            hlo[:, at] = lo

        @pl.when(q == 0)
        def _():
            hhi[pl.ds(0, NB), :] = ghi_ref[...]
            hlo[pl.ds(0, NB), :] = glo_ref[...]

    def puts(step, slot):
        return [
            pltpu.make_async_copy(
                stage.at[slot, :, pl.ds(c * 128, 128)],
                out_ref.at[pl.ds(pl.multiple_of(step * MB, MB), MB), c, :],
                sem.at[slot, c],
            )
            for c in range(8)
        ]

    slot = g % 2

    @pl.when(g >= 2)
    def _():
        for copy in puts(g - 2, slot):
            copy.wait()

    ft = f[pl.ds(pl.multiple_of(g * MB, MB), MB), :]
    for c in range(4):
        at = pl.ds(c * NB, NB)
        stage[slot, :, at] = dot(ft, hhi[at, :], NT) + dot(ft, hlo[at, :], NT)

    @pl.when((g == 0) & (p == 0))
    def _():
        for c in range(4):
            at = pl.ds(c * NB, NB)
            stage[0, :NB, at] = dot(f[:NB, :], a[at, :], NT)

    row = lax.broadcasted_iota(jnp.int32, (NB, NB), 0)
    col = lax.broadcasted_iota(jnp.int32, (NB, NB), 1)
    for t in range(MB // NB):
        r = g * (MB // NB) + t
        for c in range(4):
            @pl.when((p == q % 8) & (r == 2 * c + q // 8))
            def _():
                shift = shift_ref[pl.ds(r, 1), :]
                stage[slot, t * NB:t * NB + NB, c * NB:c * NB + NB] += jnp.where(row == col, shift, 0.0)

    @pl.when((g == 0) & (p == 0) & (q == 0))
    def _():
        stage[0, :NB, :NB] = chol_ref[...].T

    for copy in puts(g, slot):
        copy.start()

    @pl.when(g == STEPS - 1)
    def _():
        for copy in puts(g - 1, 1 - slot):
            copy.wait()
        for copy in puts(g, slot):
            copy.wait()


def tail(at, mine, theirs, cols, lead, other, shift, chol):
    vm = pl.BlockSpec(memory_space=pltpu.VMEM)
    return pl.pallas_call(
        tail_kernel,
        grid=(STEPS,),
        out_shape=jax.ShapeDtypeStruct((TILES * NB, 8, 128), f32),
        in_specs=[pl.BlockSpec(memory_space=pltpu.SMEM)] + [vm] * 16,
        out_specs=pl.BlockSpec(memory_space=pl.ANY),
        scratch_shapes=[
            pltpu.VMEM((TILES * NB, R), bf16),
            pltpu.VMEM((4 * NB, R), bf16),
            pltpu.VMEM((4 * NB, R), bf16),
            pltpu.VMEM((4 * NB, R), bf16),
            pltpu.VMEM((NB, R), bf16),
            pltpu.VMEM((2, NB, NB), bf16),
            pltpu.VMEM((NB, R), bf16),
            pltpu.VMEM((NB, R), bf16),
            pltpu.VMEM((2, MB, 4 * NB), f32),
            pltpu.SemaphoreType.DMA((2, 8)),
        ],
        compiler_params=pltpu.CompilerParams(vmem_limit_bytes=48 << 20),
    )(at, *mine, *theirs, *cols, lead, other, shift, chol)


def local(factors, shift):
    both = ("prow", "pcol")
    p = lax.axis_index("prow")
    q = lax.axis_index("pcol")
    core = q % 2
    own = factors[0]

    def send(value, pairs):
        return lax.ppermute(value, both, pairs)

    def after(value, *others):
        return lax.optimization_barrier((value, *others))[0]

    at = jnp.stack([p, q])
    to_core = moves(swap_core)

    def spread(lead, pairs):
        a, b, c = [send(lead, to) for to in pairs]
        return lead + (a + b + c)

    def star(piece, axis):
        return [piece] + [send(piece, moves(lambda at: hop(at, axis, d))) for d in (1, 3, 2)]

    rounds = spread_rounds()
    chol, lead = factor(at, own, send(own, to_core), shift[:, :NB])
    piece = send(own, to_columns())
    mine = star(jnp.stack([own, send(own, moves(swap_zl))]), "x")
    lead, piece, mine[1], mine[2] = lax.optimization_barrier((lead, piece, mine[1], mine[2]))
    pair = jnp.stack([piece, send(piece, moves(swap_zh))])
    lead, pair = lax.optimization_barrier((spread(lead, rounds[0]), pair))
    cols = star(pair, "y")
    lead = spread(lead, rounds[1])
    lead, *mine = lax.optimization_barrier((lead, *mine))
    theirs = [send(value, to_core) for value in mine]
    lead, *cols = lax.optimization_barrier((spread(lead, rounds[2]), *cols))
    out = tail(at, mine, theirs, cols, lead, send(lead, to_core), shift.reshape(TILES, NB), chol)
    return out.reshape(1, TILES * NB, 1, 4 * NB)


def solution(mesh):
    in_specs = (P("prow", "pcol", None), P("prow", None))
    out_specs = P("prow", None, "pcol", None)
    return jax.shard_map(local, mesh=mesh, in_specs=in_specs, out_specs=out_specs, check_vma=False)
```

```python
import jax
import jax.numpy as jnp
from jax import lax
from jax.experimental import pallas as pl
from jax.experimental.pallas import tpu as pltpu
from jax.sharding import PartitionSpec as P

NB = 256
OB = 32
SHARD = 128
R = 1024
TILES = 8
NPCOL = 16
MB = 512
MSG = R + 384
STEPS = TILES * NB // MB
f32 = jnp.float32
bf16 = jnp.bfloat16
HIGHEST = lax.Precision.HIGHEST
NT = (((1,), (1,)), ((), ()))
NN = (((1,), (0,)), ((), ()))
TN = (((0,), (0,)), ((), ()))


def device_of(y, zh, zl, x, core):
    return ((y * 2 + zh) * NPCOL) + (zl * 4 + x) * 2 + core


def every():
    return [
        (y, zh, zl, x, core)
        for y in range(4) for zh in range(2) for zl in range(2) for x in range(4) for core in range(2)
    ]


def moves(step):
    return [(device_of(*at), device_of(*step(*at))) for at in every()]


def moves(step):
    return [(device_of(*at), device_of(*step(at))) for at in every()]


def swap_zl(at):
    y, zh, zl, x, core = at
    return (y, zh, 1 - zl, x, core)


def swap_zh(at):
    y, zh, zl, x, core = at
    return (y, 1 - zh, zl, x, core)


def swap_core(at):
    y, zh, zl, x, core = at
    return (y, zh, zl, x, 1 - core)


def to_columns():
    pairs = []
    for p in range(8):
        for j in range(NPCOL):
            c, b, h = j // 4, j // 2 % 2, j % 2
            pairs.append((p * NPCOL + j, (2 * c + h) * NPCOL + 8 * b + p))
    return pairs


def hop(at, axis, d):
    y, zh, zl, x, core = at
    if axis == "x":
        return (y, zh, zl, (x + d) % 4, core)
    if axis == "y":
        return ((y + d) % 4, zh, zl, x, core)
    z = (zh * 2 + zl + d) % 4
    return (y, z // 2, z % 2, x, core)


def spread_rounds():
    held = {0: [(0, 0, 0, 0, 0)], 1: [(0, 0, 0, 0, 1)]}
    order = {0: "xyz", 1: "yzx"}
    rounds = []
    for step in range(3):
        ops = []
        fresh = {0: [], 1: []}
        for d in (1, 3, 2):
            pairs = []
            for core in range(2):
                for at in held[core]:
                    to = hop(at, order[core][step], d)
                    pairs.append((device_of(*at), device_of(*to)))
                    fresh[core].append(to)
            ops.append(pairs)
        for core in range(2):
            held[core] = held[core] + fresh[core]
        rounds.append(ops)
    return rounds


def split(x):
    hi = x.astype(bf16)
    return hi, (x - hi.astype(f32)).astype(bf16)


def dot(a, b, dims):
    return lax.dot_general(a, b, dims, preferred_element_type=f32)


def factor_rows(a):
    for k0 in range(0, NB, OB):
        for k in range(k0, k0 + OB, 8):
            m = k0 + OB - k
            rows = a[pl.ds(k, m), :]
            cols = [jnp.broadcast_to(rows[:, k + j:k + j + 1], (m, 128)) for j in range(8)]
            sub = lax.broadcasted_iota(jnp.int32, (m, 128), 0)
            done = []
            for j in range(8):
                scale = lax.rsqrt(jnp.broadcast_to(cols[j][j:j + 1, :], (m, 128)))
                u = cols[j] * scale
                for l in range(j + 1, 8):
                    cols[l] = cols[l] - u * jnp.broadcast_to(u[l:l + 1, :], (m, 128))
                row = jnp.concatenate(
                    [rows[j:j + 1, 128 * c:128 * c + 128] * scale[0:1, :] for c in range(4)], 1
                )
                done.append(row)
                below = jnp.where(sub > j, u, 0.0)
                rows = rows - jnp.concatenate(
                    [below * jnp.broadcast_to(row[:, 128 * c:128 * c + 128], (m, 128)) for c in range(4)], 1
                )
            a[pl.ds(k, 8), :] = jnp.concatenate(done, 0)
            if m > 8:
                a[pl.ds(k + 8, m - 8), :] = rows[8:]
        if k0 + OB < NB:
            top = a[pl.ds(k0, OB), :]
            lo = (k0 + OB) // 128 * 128
            update = lax.dot_general(
                top[:, lo:NB], top, TN, preferred_element_type=f32, precision=HIGHEST
            )
            a[pl.ds(k0 + OB, NB - k0 - OB), :] -= update[k0 + OB - lo:]


def factor_kernel(at_ref, own_ref, other_ref, shift_ref, chol_ref, msg_ref, lead, a):
    p, q = at_ref[0], at_ref[1]
    core = q % 2
    lead[pl.ds(pl.multiple_of(core * SHARD, SHARD), SHARD), :] = own_ref[...]
    lead[pl.ds(pl.multiple_of((1 - core) * SHARD, SHARD), SHARD), :] = other_ref[...]
    row = lax.broadcasted_iota(jnp.int32, (NB, NB), 0)
    col = lax.broadcasted_iota(jnp.int32, (NB, NB), 1)
    f0 = lead[...]
    a[:, :NB] = dot(f0, f0, NT) + jnp.where(row == col, shift_ref[:, :NB], 0.0)
    a[:, NB:] = jnp.where(row == col, 1.0, 0.0)
    factor_rows(a)
    chol_ref[...] = jnp.where(col >= row, a[:, :NB], 0.0)
    keep = (p == 0) & (q < 2)
    msg_ref[:, :R] = jnp.where(keep, own_ref[...], jnp.zeros_like(own_ref))
    whi, wlo = split(a[:, NB:])
    part = jnp.where(keep, jnp.where(core == 0, whi, wlo), jnp.zeros_like(whi))
    msg_ref[:, R:R + 128] = part[:128, :128]
    msg_ref[:, R + 128:R + 384] = part[128:, :]


def factor(at, own, other, shift):
    vm = pl.BlockSpec(memory_space=pltpu.VMEM)
    return pl.pallas_call(
        factor_kernel,
        out_shape=[jax.ShapeDtypeStruct((NB, NB), f32), jax.ShapeDtypeStruct((SHARD, MSG), bf16)],
        in_specs=[pl.BlockSpec(memory_space=pltpu.SMEM), vm, vm, vm],
        out_specs=[vm, vm],
        scratch_shapes=[pltpu.VMEM((NB, R), bf16), pltpu.VMEM((NB, 2 * NB), f32)],
        compiler_params=pltpu.CompilerParams(vmem_limit_bytes=32 << 20),
        cost_estimate=pl.CostEstimate(flops=20_000_000_000, bytes_accessed=1 << 20, transcendentals=0),
    )(at, own, other, shift)


def tail_kernel(at_ref, *refs):
    mine, theirs, cols = refs[0:4], refs[4:8], refs[8:12]
    lead_ref, other_ref, shift_ref, chol_ref, out_ref, f, a, hhi, hlo, f0, w, ghi_ref, glo_ref, stage, sem = refs[12:]
    p, q = at_ref[0], at_ref[1]
    y, zh = p // 2, p % 2
    zl, x, core = q // 8, q // 2 % 4, q % 2
    g = pl.program_id(0)

    def shard(n):
        return pl.ds(pl.multiple_of(n * SHARD, SHARD), SHARD)

    @pl.when(g == 0)
    def _():
        for n, d in enumerate((0, 1, 3, 2)):
            for j in range(2):
                for bufs, whose in ((mine, core), (theirs, 1 - core)):
                    tile = (zl + j) % 2 * 4 + (x + 4 - d) % 4
                    f[shard(tile * 2 + whose), :] = bufs[n][j]
                a[shard((y + 4 - d) % 4 * 2 + (zh + j) % 2), :] = cols[n][j]
        f0[pl.ds(pl.multiple_of(core * SHARD, SHARD), SHARD), :] = lead_ref[:, :R]
        f0[pl.ds(pl.multiple_of((1 - core) * SHARD, SHARD), SHARD), :] = other_ref[:, :R]
        for n, (own, other) in enumerate(((lead_ref, other_ref), (other_ref, lead_ref))):
            part = jnp.where(core == 0, own[:, R:], other[:, R:])
            w[n, :128, :128] = part[:, :128]
            w[n, :128, 128:] = jnp.zeros((128, 128), bf16)
            w[n, 128:, :] = part[:, 128:]
        ghi, glo = split(dot(w[0], f0[...], NN) + dot(w[1], f0[...], NN))
        ghi_ref[...] = ghi
        glo_ref[...] = glo
        lhi, llo = split(dot(a[...], ghi_ref[...], NT) + dot(a[...], glo_ref[...], NT))
        for k in range(4):
            at = pl.ds(k * NB, NB)
            h = a[:, at].astype(f32) - (
                dot(lhi, ghi_ref[:, at], NN) + dot(lhi, glo_ref[:, at], NN) + dot(llo, ghi_ref[:, at], NN)
            )
            hi, lo = split(h)
            hhi[:, at] = hi
            hlo[:, at] = lo

        @pl.when(q == 0)
        def _():
            hhi[pl.ds(0, NB), :] = ghi_ref[...]
            hlo[pl.ds(0, NB), :] = glo_ref[...]

    def puts(step, slot):
        return [
            pltpu.make_async_copy(
                stage.at[slot, :, pl.ds(c * 128, 128)],
                out_ref.at[pl.ds(pl.multiple_of(step * MB, MB), MB), c, :],
                sem.at[slot, c],
            )
            for c in range(8)
        ]

    slot = g % 2

    @pl.when(g >= 2)
    def _():
        for copy in puts(g - 2, slot):
            copy.wait()

    ft = f[pl.ds(pl.multiple_of(g * MB, MB), MB), :]
    for c in range(4):
        at = pl.ds(c * NB, NB)
        stage[slot, :, at] = dot(ft, hhi[at, :], NT) + dot(ft, hlo[at, :], NT)

    @pl.when((g == 0) & (p == 0))
    def _():
        for c in range(4):
            at = pl.ds(c * NB, NB)
            stage[0, :NB, at] = dot(f[:NB, :], a[at, :], NT)

    row = lax.broadcasted_iota(jnp.int32, (NB, NB), 0)
    col = lax.broadcasted_iota(jnp.int32, (NB, NB), 1)
    for t in range(MB // NB):
        r = g * (MB // NB) + t
        for c in range(4):
            @pl.when((p == q % 8) & (r == 2 * c + q // 8))
            def _():
                shift = shift_ref[:, pl.ds(pl.multiple_of(r * NB, NB), NB)]
                stage[slot, t * NB:t * NB + NB, c * NB:c * NB + NB] += jnp.where(row == col, shift, 0.0)

    @pl.when((g == 0) & (p == 0) & (q == 0))
    def _():
        stage[0, :NB, :NB] = chol_ref[...].T

    for copy in puts(g, slot):
        copy.start()

    @pl.when(g == STEPS - 1)
    def _():
        for copy in puts(g - 1, 1 - slot):
            copy.wait()
        for copy in puts(g, slot):
            copy.wait()


def tail(at, mine, theirs, cols, lead, other, shift, chol):
    vm = pl.BlockSpec(memory_space=pltpu.VMEM)
    return pl.pallas_call(
        tail_kernel,
        grid=(STEPS,),
        out_shape=jax.ShapeDtypeStruct((TILES * NB, 8, 128), f32),
        in_specs=[pl.BlockSpec(memory_space=pltpu.SMEM)] + [vm] * 16,
        out_specs=pl.BlockSpec(memory_space=pl.ANY),
        scratch_shapes=[
            pltpu.VMEM((TILES * NB, R), bf16),
            pltpu.VMEM((4 * NB, R), bf16),
            pltpu.VMEM((4 * NB, R), bf16),
            pltpu.VMEM((4 * NB, R), bf16),
            pltpu.VMEM((NB, R), bf16),
            pltpu.VMEM((2, NB, NB), bf16),
            pltpu.VMEM((NB, R), bf16),
            pltpu.VMEM((NB, R), bf16),
            pltpu.VMEM((2, MB, 4 * NB), f32),
            pltpu.SemaphoreType.DMA((2, 8)),
        ],
        compiler_params=pltpu.CompilerParams(vmem_limit_bytes=48 << 20),
    )(at, *mine, *theirs, *cols, lead, other, shift, chol)


def local(factors, shift):
    both = ("prow", "pcol")
    p = lax.axis_index("prow")
    q = lax.axis_index("pcol")
    core = q % 2
    own = factors[0]

    def send(value, pairs):
        return lax.ppermute(value, both, pairs)

    def after(value, *others):
        return lax.optimization_barrier((value, *others))[0]

    at = jnp.stack([p, q])
    to_core = moves(swap_core)

    def spread(lead, pairs):
        a, b, c = [send(lead, to) for to in pairs]
        return lead + (a + b + c)

    def star(piece, axis):
        return [piece] + [send(piece, moves(lambda at: hop(at, axis, d))) for d in (1, 3, 2)]

    rounds = spread_rounds()
    chol, lead = factor(at, own, send(own, to_core), shift)
    piece = send(own, to_columns())
    mine = star(jnp.stack([own, send(own, moves(swap_zl))]), "x")
    lead, piece, mine[1], mine[2] = lax.optimization_barrier((lead, piece, mine[1], mine[2]))
    pair = jnp.stack([piece, send(piece, moves(swap_zh))])
    lead, pair = lax.optimization_barrier((spread(lead, rounds[0]), pair))
    cols = star(pair, "y")
    lead = spread(lead, rounds[1])
    lead, *mine = lax.optimization_barrier((lead, *mine))
    theirs = [send(value, to_core) for value in mine]
    lead, *cols = lax.optimization_barrier((spread(lead, rounds[2]), *cols))
    out = tail(at, mine, theirs, cols, lead, send(lead, to_core), shift, chol)
    return out.reshape(1, TILES * NB, 1, 4 * NB)


def solution(mesh):
    in_specs = (P("prow", "pcol", None), P("prow", None))
    out_specs = P("prow", None, "pcol", None)
    return jax.shard_map(local, mesh=mesh, in_specs=in_specs, out_specs=out_specs, check_vma=False)
```

```python
import jax
import jax.numpy as jnp
from jax import lax
from jax.experimental import pallas as pl
from jax.experimental.pallas import tpu as pltpu
from jax.sharding import PartitionSpec as P

NB = 256
OB = 32
SHARD = 128
R = 1024
TILES = 8
NPCOL = 16
MB = 512
OFFSETS = (0, 1, 3, 2)
MSG = R + 384
f32 = jnp.float32
bf16 = jnp.bfloat16
HIGHEST = lax.Precision.HIGHEST
NT = (((1,), (1,)), ((), ()))
NN = (((1,), (0,)), ((), ()))
TN = (((0,), (0,)), ((), ()))


def device_of(y, zh, zl, x, core):
    return ((y * 2 + zh) * NPCOL) + (zl * 4 + x) * 2 + core


def every():
    return [
        (y, zh, zl, x, core)
        for y in range(4) for zh in range(2) for zl in range(2) for x in range(4) for core in range(2)
    ]


def moves(step):
    return [(device_of(*at), device_of(*step(*at))) for at in every()]


def moves(step):
    return [(device_of(*at), device_of(*step(at))) for at in every()]


def swap_zl(at):
    y, zh, zl, x, core = at
    return (y, zh, 1 - zl, x, core)


def swap_zh(at):
    y, zh, zl, x, core = at
    return (y, 1 - zh, zl, x, core)


def swap_core(at):
    y, zh, zl, x, core = at
    return (y, zh, zl, x, 1 - core)


def to_columns():
    pairs = []
    for p in range(8):
        for j in range(NPCOL):
            c, b, h = j // 4, j // 2 % 2, j % 2
            pairs.append((p * NPCOL + j, (2 * c + h) * NPCOL + 8 * b + p))
    return pairs


def hop(at, axis, d):
    y, zh, zl, x, core = at
    if axis == "x":
        return (y, zh, zl, (x + d) % 4, core)
    if axis == "y":
        return ((y + d) % 4, zh, zl, x, core)
    z = (zh * 2 + zl + d) % 4
    return (y, z // 2, z % 2, x, core)


def spread_rounds():
    held = {0: [(0, 0, 0, 0, 0)], 1: [(0, 0, 0, 0, 1)]}
    order = {0: "yzx", 1: "zxy"}
    rounds = []
    for step in range(3):
        ops = []
        fresh = {0: [], 1: []}
        for d in (1, 3, 2):
            pairs = []
            for core in range(2):
                for at in held[core]:
                    to = hop(at, order[core][step], d)
                    pairs.append((device_of(*at), device_of(*to)))
                    fresh[core].append(to)
            ops.append(pairs)
        for core in range(2):
            held[core] = held[core] + fresh[core]
        rounds.append(ops)
    return rounds


def split(x):
    hi = x.astype(bf16)
    return hi, (x - hi.astype(f32)).astype(bf16)


def dot(a, b, dims):
    return lax.dot_general(a, b, dims, preferred_element_type=f32)


def factor_rows(a):
    for k0 in range(0, NB, OB):
        for k in range(k0, k0 + OB, 8):
            m = k0 + OB - k
            rows = a[pl.ds(k, m), :]
            cols = [jnp.broadcast_to(rows[:, k + j:k + j + 1], (m, 128)) for j in range(8)]
            sub = lax.broadcasted_iota(jnp.int32, (m, 128), 0)
            done = []
            for j in range(8):
                scale = lax.rsqrt(jnp.broadcast_to(cols[j][j:j + 1, :], (m, 128)))
                u = cols[j] * scale
                for l in range(j + 1, 8):
                    cols[l] = cols[l] - u * jnp.broadcast_to(u[l:l + 1, :], (m, 128))
                row = jnp.concatenate(
                    [rows[j:j + 1, 128 * c:128 * c + 128] * scale[0:1, :] for c in range(4)], 1
                )
                done.append(row)
                below = jnp.where(sub > j, u, 0.0)
                rows = rows - jnp.concatenate(
                    [below * jnp.broadcast_to(row[:, 128 * c:128 * c + 128], (m, 128)) for c in range(4)], 1
                )
            a[pl.ds(k, 8), :] = jnp.concatenate(done, 0)
            if m > 8:
                a[pl.ds(k + 8, m - 8), :] = rows[8:]
        if k0 + OB < NB:
            top = a[pl.ds(k0, OB), :]
            lo = (k0 + OB) // 128 * 128
            update = lax.dot_general(
                top[:, lo:NB], top, TN, preferred_element_type=f32, precision=HIGHEST
            )
            a[pl.ds(k0 + OB, NB - k0 - OB), :] -= update[k0 + OB - lo:]


def factor_kernel(at_ref, own_ref, other_ref, shift_ref, chol_ref, msg_ref, lead, a):
    p, q = at_ref[0], at_ref[1]
    core = q % 2
    lead[pl.ds(pl.multiple_of(core * SHARD, SHARD), SHARD), :] = own_ref[...]
    lead[pl.ds(pl.multiple_of((1 - core) * SHARD, SHARD), SHARD), :] = other_ref[...]
    row = lax.broadcasted_iota(jnp.int32, (NB, NB), 0)
    col = lax.broadcasted_iota(jnp.int32, (NB, NB), 1)
    f0 = lead[...]
    a[:, :NB] = dot(f0, f0, NT) + jnp.where(row == col, shift_ref[:, :NB], 0.0)
    a[:, NB:] = jnp.where(row == col, 1.0, 0.0)
    factor_rows(a)
    chol_ref[...] = jnp.where(col >= row, a[:, :NB], 0.0)
    keep = (p == 0) & (q < 2)
    msg_ref[:, :R] = jnp.where(keep, own_ref[...], jnp.zeros_like(own_ref))
    whi, wlo = split(a[:, NB:])
    part = jnp.where(keep, jnp.where(core == 0, whi, wlo), jnp.zeros_like(whi))
    msg_ref[:, R:R + 128] = part[:128, :128]
    msg_ref[:, R + 128:R + 384] = part[128:, :]


def factor(at, own, other, shift):
    vm = pl.BlockSpec(memory_space=pltpu.VMEM)
    return pl.pallas_call(
        factor_kernel,
        out_shape=[jax.ShapeDtypeStruct((NB, NB), f32), jax.ShapeDtypeStruct((SHARD, MSG), bf16)],
        in_specs=[pl.BlockSpec(memory_space=pltpu.SMEM), vm, vm, vm],
        out_specs=[vm, vm],
        scratch_shapes=[pltpu.VMEM((NB, R), bf16), pltpu.VMEM((NB, 2 * NB), f32)],
        compiler_params=pltpu.CompilerParams(vmem_limit_bytes=32 << 20),
        cost_estimate=pl.CostEstimate(flops=20_000_000_000, bytes_accessed=1 << 20, transcendentals=0),
    )(at, own, other, shift)


def rows_of(mine, theirs, n):
    return jnp.concatenate([mine[n][0], theirs[n][0], mine[n][1], theirs[n][1]], 0)


def base_kernel(*refs):
    mine, theirs, cols_ref, out_ref = refs[0:4], refs[4:8], refs[8], refs[9]
    cols = jnp.concatenate([cols_ref[0], cols_ref[1]], 0)
    for n in range(4):
        out_ref[n * MB:n * MB + MB, :] = dot(rows_of(mine, theirs, n), cols, NT)


def base(mine, theirs, cols):
    vm = pl.BlockSpec(memory_space=pltpu.VMEM)
    return pl.pallas_call(
        base_kernel,
        out_shape=jax.ShapeDtypeStruct((TILES * NB, NB), f32),
        in_specs=[vm] * 9,
        out_specs=vm,
        compiler_params=pltpu.CompilerParams(vmem_limit_bytes=16 << 20),
        cost_estimate=pl.CostEstimate(flops=2 * TILES * NB * NB * R, bytes_accessed=8 << 20, transcendentals=0),
    )(*mine, *theirs, cols)


def tail_kernel(at_ref, *refs):
    mine, theirs, cols, bases = refs[0:4], refs[4:8], refs[8:12], refs[12:16]
    lead_ref, other_ref, shift_ref, chol_ref, out_ref, f0, w, ghi_ref, glo_ref, lq, stage, sem = refs[16:]
    p, q = at_ref[0], at_ref[1]
    y, zh = p // 2, p % 2
    zl, x, core = q // 8, q // 2 % 4, q % 2

    f0[pl.ds(pl.multiple_of(core * SHARD, SHARD), SHARD), :] = lead_ref[:, :R]
    f0[pl.ds(pl.multiple_of((1 - core) * SHARD, SHARD), SHARD), :] = other_ref[:, :R]
    for n, (own, other) in enumerate(((lead_ref, other_ref), (other_ref, lead_ref))):
        part = jnp.where(core == 0, own[:, R:], other[:, R:])
        w[n, :128, :128] = part[:, :128]
        w[n, :128, 128:] = jnp.zeros((128, 128), bf16)
        w[n, 128:, :] = part[:, 128:]
    ghi, glo = split(dot(w[0], f0[...], NN) + dot(w[1], f0[...], NN))
    ghi_ref[...] = ghi
    glo_ref[...] = glo

    def panel(factor_rows):
        return dot(factor_rows, ghi_ref[...], NT) + dot(factor_rows, glo_ref[...], NT)

    for m in range(4):
        hi, lo = split(panel(jnp.concatenate([cols[m][0], cols[m][1]], 0)))
        lq[m] = jnp.concatenate([hi, lo, hi], 1)

    row = lax.broadcasted_iota(jnp.int32, (NB, NB), 0)
    col = lax.broadcasted_iota(jnp.int32, (NB, NB), 1)
    tile = [[(zl + j) % 2 * 4 + (x + 4 - d) % 4 for j in range(2)] for d in OFFSETS]

    def puts(n):
        return [
            pltpu.make_async_copy(
                stage.at[n % 2, pl.ds(j * NB, NB), pl.ds(c * 128, 128)],
                out_ref.at[pl.ds(pl.multiple_of(tile[n][j] * NB, NB), NB), c, :],
                sem.at[n % 2, j, c],
            )
            for j in range(2)
            for c in range(8)
        ]

    def place(n, j, own):
        whose = core if own == 0 else 1 - core
        return n % 2, pl.ds(pl.multiple_of(j * NB + whose * SHARD, SHARD), SHARD)

    for n in range(4):
        l = panel(rows_of(mine, theirs, n))
        hi, lo = split(l)
        lcat = jnp.concatenate([hi, hi, lo], 1)
        if n >= 2:
            for copy in puts(n - 2):
                copy.wait()

        def store(value, m, j, own):
            slot, at = place(n, j, own)
            k = (2 * j + own) * SHARD
            for h in range(2):
                c = (y + 4 - OFFSETS[m]) % 4 * 2 + (zh + h) % 2
                cat = pl.ds(pl.multiple_of(c * 128, 128), 128)
                stage[slot, at, cat] = value[k:k + SHARD, h * 128:h * 128 + 128]

        for m in range(4):
            value = bases[m][n * MB:n * MB + MB, :] - dot(lcat, lq[m], NT)
            for j in range(2):
                for own in range(2):
                    store(value, m, j, own)
        for j in range(2):
            r = tile[n][j]
            at = pl.ds(j * NB, NB)

            @pl.when(q == 0)
            def _():
                for own in range(2):
                    slot, rows = place(n, j, own)
                    k = (2 * j + own) * SHARD
                    stage[slot, rows, :NB] = l[k:k + SHARD, :]

            @pl.when((p == 0) & (r == 0))
            def _():
                for m in range(4):
                    for own in range(2):
                        store(bases[m][n * MB:n * MB + MB, :], m, j, own)

            @pl.when((p == q % 8) & (r % 2 == q // 8))
            def _():
                c = pl.ds(pl.multiple_of(r // 2 * NB, NB), NB)
                stage[n % 2, at, c] += jnp.where(row == col, shift_ref[:, pl.ds(pl.multiple_of(r * NB, NB), NB)], 0.0)

            @pl.when((p == 0) & (q == 0) & (r == 0))
            def _():
                stage[n % 2, at, :NB] = chol_ref[...].T

        for copy in puts(n):
            copy.start()
    for n in range(2, 4):
        for copy in puts(n):
            copy.wait()


def tail(at, mine, theirs, cols, bases, lead, other, shift, chol):
    vm = pl.BlockSpec(memory_space=pltpu.VMEM)
    return pl.pallas_call(
        tail_kernel,
        out_shape=jax.ShapeDtypeStruct((TILES * NB, 8, 128), f32),
        in_specs=[pl.BlockSpec(memory_space=pltpu.SMEM)] + [vm] * 20,
        out_specs=pl.BlockSpec(memory_space=pl.ANY),
        scratch_shapes=[
            pltpu.VMEM((NB, R), bf16),
            pltpu.VMEM((2, NB, NB), bf16),
            pltpu.VMEM((NB, R), bf16),
            pltpu.VMEM((NB, R), bf16),
            pltpu.VMEM((4, NB, 3 * NB), bf16),
            pltpu.VMEM((2, MB, 4 * NB), f32),
            pltpu.SemaphoreType.DMA((2, 2, 8)),
        ],
        compiler_params=pltpu.CompilerParams(vmem_limit_bytes=24 << 20),
    )(at, *mine, *theirs, *cols, *bases, lead, other, shift, chol)


def local(factors, shift):
    both = ("prow", "pcol")
    p = lax.axis_index("prow")
    q = lax.axis_index("pcol")
    core = q % 2
    own = factors[0]

    def send(value, pairs):
        return lax.ppermute(value, both, pairs)

    def after(value, *others):
        return lax.optimization_barrier((value, *others))[0]

    at = jnp.stack([p, q])
    to_core = moves(swap_core)

    def spread(lead, pairs):
        a, b, c = [send(lead, to) for to in pairs]
        return lead + (a + b + c)

    def star(piece, axis):
        return [piece] + [send(piece, moves(lambda at: hop(at, axis, d))) for d in OFFSETS[1:]]

    rounds = spread_rounds()
    chol, lead = factor(at, own, send(own, to_core), shift)
    piece = send(own, to_columns())
    mine = star(jnp.stack([own, send(own, moves(swap_zl))]), "x")
    lead, piece, mine[1], mine[2] = lax.optimization_barrier((lead, piece, mine[1], mine[2]))
    pair = jnp.stack([piece, send(piece, moves(swap_zh))])
    lead, pair = lax.optimization_barrier((spread(lead, rounds[0]), pair))
    cols = star(pair, "y")
    lead = after(spread(lead, rounds[1]), mine[3], *cols[1:])
    theirs = [send(value, to_core) for value in mine]
    bases = [base(mine, theirs, value) for value in cols]
    a, b, c = [send(lead, to) for to in rounds[2]]
    lead = after(lead, *bases) + (a + b + c)
    other = send(lead, to_core)
    out = tail(at, mine, theirs, cols, bases, lead, other, shift, chol)
    return out.reshape(1, TILES * NB, 1, 4 * NB)


def solution(mesh):
    in_specs = (P("prow", "pcol", None), P("prow", None))
    out_specs = P("prow", None, "pcol", None)
    return jax.shard_map(local, mesh=mesh, in_specs=in_specs, out_specs=out_specs, check_vma=False)
```
